256 devices in a mesh: row: 32 (over x, z), col: 8 (over y, core).
Axes of the slice: x: 4, y: 4, z: 8, core: 2. Of those that a mesh axis runs over, the one named last changes fastest.
Arguments:
- slab: float32 [6, 8192, 4, 2048], P(None, 'row', None, 'col'), may hold values from -18 to 27, as said below
Outputs:
- factored: float32 [6, 8192, 4, 2048], P(None, 'row', None, 'col')
The draws below stay inside these ranges and needn't reach their ends.
Inputs may be any that keep to these rules, and one draw needn't show every extreme that they name: `slab`: read as a matrix, its leading 2 * 256 rows and columns, made symmetric from their lower triangle, are positive definite.
All inputs are finite; a program needn't handle non-finite values.
Results may differ from the reference program's by a relative error of at most 0.0022.
Values may be sent and summed in bfloat16 or wider, within the bound.
No kernel may reach another device: no remote copies, remote signals or barrier semaphores. Data moves between devices by JAX's collectives and lax.ppermute only.
A program may use at most 128 MiB of HBM per device.

```python
import math
import jax
import jax.numpy as jnp
from jax import lax

NB = 256
RBL = 6
CBL = 4
ORDER = 49152
WIDTH = 8192
N_ROW = 32
N_COL = 8


def draw_slab(key, part):
    key = jax.random.fold_in(key, 11)
    place_key, scale_key, radius_key, angle_key, phase_key = jax.random.split(key, 5)
    feature_count = 1536
    places = jax.random.uniform(place_key, (2, ORDER), jnp.float32, 0.0, 4.0)
    scales = jnp.exp(jax.random.uniform(scale_key, (ORDER,), jnp.float32, math.log(0.3), math.log(3.0)))
    radius = jnp.exp(jax.random.uniform(radius_key, (feature_count,), jnp.float32, math.log(3.0), math.log(40.0)))
    angle = jax.random.uniform(angle_key, (feature_count,), jnp.float32, -math.pi, math.pi)
    phase = jax.random.uniform(phase_key, (feature_count,), jnp.float32, -math.pi, math.pi)
    waves = places[0][:, None] * (radius * jnp.cos(angle))[None, :] + places[1][:, None] * (radius * jnp.sin(angle))[None, :] + phase[None, :]
    features = jnp.cos(waves) * math.sqrt(2.0 / feature_count)
    spectral = jnp.dot(features, features[:WIDTH].T, precision=lax.Precision.HIGHEST, preferred_element_type=jnp.float32)
    across = places[0][:, None] - places[0][None, :WIDTH]
    down = places[1][:, None] - places[1][None, :WIDTH]
    distance = jnp.sqrt(across * across + down * down)
    row_ids = lax.broadcasted_iota(jnp.int32, (ORDER, WIDTH), 0)
    col_ids = lax.broadcasted_iota(jnp.int32, (ORDER, WIDTH), 1)
    kernel = 0.5 * jnp.exp(-distance) + spectral + jnp.where(row_ids == col_ids, 0.1, 0.0)
    entries = kernel * scales[:, None] * scales[None, :WIDTH]
    return entries.reshape(RBL, N_ROW * NB, CBL, N_COL * NB)


def setup_inputs(seed: int = 0) -> dict:
    key_of = jax.random.split(jax.random.key(seed), 2)
    return {
        "slab": draw_slab(jax.random.fold_in(key_of[1], 71), 0),
    }


def symmetric_lower(square):
    return jnp.tril(square) + jnp.tril(square, -1).T

def factor_column(column, start, panel_width):
    pivot_block = symmetric_lower(column[start:start + panel_width])
    cholesky_part = jnp.linalg.cholesky(pivot_block)
    solved = lax.linalg.triangular_solve(cholesky_part, column, left_side=False, lower=True, transpose_a=True)
    row_ids = jnp.arange(column.shape[0], dtype=jnp.int32)[:, None]
    solved = jnp.where(row_ids < start, jnp.zeros_like(solved), solved)
    return solved.at[start:start + panel_width].set(cholesky_part)

def reference(slab):
    panel_width = NB
    matrix = slab.reshape(ORDER, WIDTH)
    first = factor_column(matrix[:, :panel_width], 0, panel_width)
    first_wide = first.astype(jnp.bfloat16).astype(jnp.float32)
    column = matrix[:, panel_width:2 * panel_width] - jnp.dot(first_wide.astype(jnp.float32), first_wide[panel_width:2 * panel_width].T.astype(jnp.float32), precision=lax.Precision.HIGHEST, preferred_element_type=jnp.float32)
    second = factor_column(column, panel_width, panel_width)
    second_wide = second.astype(jnp.bfloat16).astype(jnp.float32)
    combined = jnp.concatenate([first_wide, second_wide], axis=1)
    update = jnp.dot(combined[2 * panel_width:].astype(jnp.float32), combined[2 * panel_width:WIDTH].T.astype(jnp.float32), precision=lax.Precision.HIGHEST, preferred_element_type=jnp.float32)
    lower_rows = matrix[2 * panel_width:, 2 * panel_width:] - update
    remainder = jnp.concatenate([matrix[:2 * panel_width, 2 * panel_width:], lower_rows], axis=0)
    output = jnp.concatenate([first, second, remainder], axis=1)
    return output.reshape(RBL, N_ROW * NB, CBL, N_COL * NB)
```

```python
import functools
import jax
import jax.numpy as jnp
from jax import lax
from jax.experimental import pallas as pl
from jax.experimental.pallas import tpu as pltpu
from jax.sharding import Mesh
from jax.sharding import PartitionSpec as P

NB = 256
STEP = 8
HALF = 128
X, Z, Y, CORE = 4, 8, 4, 2
RBL, CBL = 6, 4
EXACT = lax.Precision.HIGHEST
PLANE = ("x", "y", "core")


def times_transposed(left, right, precision=None):
    return lax.dot_general(
        left, right, (((1,), (1,)), ((), ())), precision=precision, preferred_element_type=jnp.float32
    )


def lane_of(tile, lane):
    return jnp.broadcast_to(tile[:, lane:lane + 1], (STEP, HALF))


def row_of(tile, row):
    return jnp.broadcast_to(tile[row:row + 1, :], tile.shape)


def twice(value):
    return jnp.concatenate([value, value], axis=1)


def symmetric(value):
    rows = lax.broadcasted_iota(jnp.int32, (NB, NB), 0)
    cols = lax.broadcasted_iota(jnp.int32, (NB, NB), 1)
    return jnp.where(rows >= cols, value, value.T)


def factor(work, inverse_ref, upper_ref):
    lanes = lax.broadcasted_iota(jnp.int32, (STEP, NB), 1)
    rows = lax.broadcasted_iota(jnp.int32, (STEP, NB), 0)
    for step in range(NB // STEP):
        j = step * STEP
        half = j // HALF * HALF
        tile = work[j:j + STEP, :]
        diag = tile[:, half:half + HALF]
        cols = [lane_of(diag, j - half + k) for k in range(STEP)]
        left = [[row_of(cols[k], s) if k <= s else None for k in range(STEP)] for s in range(STEP)]
        low = [[None] * STEP for _ in range(STEP)]
        root = [None] * STEP
        inside = (lanes >= j) & (lanes < j + STEP)
        right = [
            jnp.where(inside, jnp.where(lanes == j + i, 1.0, 0.0), row_of(tile, i)) for i in range(STEP)
        ]
        solved = [None] * STEP
        for k in range(STEP):
            root[k] = lax.rsqrt(left[k][k])
            for s in range(k + 1, STEP):
                low[s][k] = left[s][k] * root[k]
            for s in range(k + 1, STEP):
                for m in range(k + 1, s + 1):
                    left[s][m] = left[s][m] - low[s][k] * low[m][k]
            solved[k] = right[k] * twice(root[k])
            for s in range(k + 1, STEP):
                right[s] = right[s] - twice(low[s][k]) * solved[k]
        weights = [None] * STEP
        for i in range(STEP - 1, -1, -1):
            total = solved[i]
            for s in range(i + 1, STEP):
                total = total - twice(low[s][i]) * weights[s]
            weights[i] = total * twice(root[i])
        for t in range(step + 1, NB // STEP):
            other = work[t * STEP:(t + 1) * STEP, :]
            side = other[:, half:half + HALF]
            total = jnp.where(inside, 0.0, other)
            for i in range(STEP):
                total = total - twice(lane_of(side, j - half + i)) * weights[i]
            work[t * STEP:(t + 1) * STEP, :] = total
        final = solved[0]
        for i in range(1, STEP):
            final = jnp.where(rows == i, solved[i], final)
        block = jnp.zeros((STEP, NB), jnp.float32)
        for i in range(STEP):
            for s in range(i, STEP):
                value = low[s][i] if s > i else left[i][i] * root[i]
                block = jnp.where((rows == i) & (lanes == j + s), twice(value), block)
        inverse_ref[j:j + STEP, :] = jnp.where(lanes < j + STEP, final, 0.0)
        upper_ref[j:j + STEP, :] = jnp.where(lanes >= j + STEP, final, block)


def leading_kernel(pieces, inverse, lower, first_low, source, upper, work):
    for part in range(2):
        source[part] = pieces[:, 2 * part].reshape(NB, NB)

    @pl.loop(0, 2)
    def _(panel):
        work[...] = symmetric(source[panel])
        factor(work, inverse.at[panel], upper)
        lower[panel] = upper[...].T

        @pl.when(panel == 0)
        def _():
            rows = times_transposed(pieces[:, 1].reshape(NB, NB), inverse[0], EXACT).astype(jnp.bfloat16)
            first_low[...] = rows
            source[1] = source[1] - times_transposed(rows, rows)


def factor_leading(pieces):
    pair = jax.ShapeDtypeStruct((2, NB, NB), jnp.float32)
    whole = pl.BlockSpec(memory_space=pltpu.VMEM)
    return pl.pallas_call(
        leading_kernel,
        out_shape=[pair, pair, jax.ShapeDtypeStruct((NB, NB), jnp.bfloat16)],
        in_specs=[whole],
        out_specs=[whole] * 3,
        scratch_shapes=[
            pltpu.VMEM((2, NB, NB), jnp.float32),
            pltpu.VMEM((NB, NB), jnp.float32),
            pltpu.VMEM((NB, NB), jnp.float32),
        ],
        compiler_params=pltpu.CompilerParams(vmem_limit_bytes=40 * 2**20),
        cost_estimate=pl.CostEstimate(flops=2**31, bytes_accessed=2**21, transcendentals=512),
        name="leading",
    )(pieces)


def right_kernel(raw, inverse, first_low, out):
    first = times_transposed(raw[0], inverse[0], EXACT).astype(jnp.bfloat16)
    column = raw[1] - times_transposed(first, first_low[...])
    second = times_transposed(column, inverse[1], EXACT).astype(jnp.bfloat16)
    out[:, :NB] = first
    out[:, NB:] = second


def right_rows(raw, inverse, first_low):
    whole = pl.BlockSpec(memory_space=pltpu.VMEM)
    return pl.pallas_call(
        right_kernel,
        out_shape=jax.ShapeDtypeStruct((NB // Z, 2 * NB), jnp.bfloat16),
        in_specs=[whole] * 3,
        out_specs=whole,
        name="right_rows",
    )(raw, inverse, first_low)


def update_kernel(index, slab, left_first, left_second, right, inverse, lower, first_low, out):
    row_block = pl.program_id(0) * (X * Z) + index[0]
    col_index = index[1]
    first = times_transposed(left_first[0], inverse[0], EXACT)
    first = jnp.where(row_block == 0, lower[0], first)
    first_bf16 = first.astype(jnp.bfloat16)
    column = left_second[0] - times_transposed(first_bf16, first_low[...])
    second = times_transposed(column, inverse[1], EXACT)
    second = jnp.where(row_block == 1, lower[1], jnp.where(row_block == 0, 0.0, second))
    both = jnp.concatenate([first_bf16, second.astype(jnp.bfloat16)], axis=1)
    for m in range(CBL):
        base = slab[0, :, m, :]
        live = (row_block >= 2) & (m * (Y * CORE) + col_index >= 2)
        value = base - jnp.where(live, times_transposed(both, right[m]), 0.0)
        if m == 0:
            value = jnp.where(col_index == 0, first, jnp.where(col_index == 1, second, value))
        out[0, :, m, :] = value


def update(index, slab, left_first, left_second, right, inverse, lower, first_low):
    fixed = lambda *shape: pl.BlockSpec(shape, lambda b, _: (0,) * len(shape))
    slab_spec = pl.BlockSpec((1, NB, CBL, NB), lambda b, _: (b, 0, 0, 0))
    rows_spec = pl.BlockSpec((1, NB, NB), lambda b, _: (b, 0, 0))
    return pl.pallas_call(
        update_kernel,
        grid_spec=pltpu.PrefetchScalarGridSpec(
            num_scalar_prefetch=1,
            grid=(RBL,),
            in_specs=[
                slab_spec, rows_spec, rows_spec, fixed(CBL, NB, 2 * NB),
                fixed(2, NB, NB), fixed(2, NB, NB), fixed(NB, NB),
            ],
            out_specs=slab_spec,
        ),
        out_shape=jax.ShapeDtypeStruct(slab.shape, jnp.float32),
        compiler_params=pltpu.CompilerParams(vmem_limit_bytes=40 * 2**20),
        name="update",
    )(index, slab, left_first, left_second, right, inverse, lower, first_low)


def per_device(slab):
    x, z = lax.axis_index("x"), lax.axis_index("z")
    y, core = lax.axis_index("y"), lax.axis_index("core")
    index = jnp.stack([x * Z + z, y * CORE + core]).astype(jnp.int32)
    own = slab[:, :, 0, :]
    top = own[0]

    def place(k):
        pairs = [
            ((zz * Y + 0) * CORE + k, (zz * Y + zz // CORE) * CORE + zz % CORE) for zz in range(Z)
        ]
        return lax.ppermute(top, ("z", "y", "core"), pairs)

    placed = jnp.stack([place(0), place(1)])

    half = RBL // 2
    to_one = lax.ppermute(own, "y", [(0, 1)])
    to_three = lax.ppermute(own, "y", [(0, 3)])
    to_two = jnp.concatenate(
        [lax.ppermute(to_one[:half], "y", [(1, 2)]), lax.ppermute(to_three[half:], "y", [(3, 2)])]
    )
    mine = jnp.where(y == 0, own, jnp.where(y == 1, to_one, jnp.where(y == 3, to_three, to_two)))
    other = lax.ppermute(mine, "core", [(0, 1), (1, 0)])
    left_first = jnp.where(core == 0, mine, other)
    left_second = jnp.where(core == 0, other, mine)

    scattered = lax.all_to_all(top.reshape(X * Y * CORE, STEP, NB), PLANE, 0, 0)[:2]
    chunk = NB // Z
    to_z = jnp.concatenate(
        [
            jnp.broadcast_to(scattered.reshape(1, 2 * STEP, NB), (Z, 2 * STEP, NB)),
            placed.reshape(2, Z, chunk, NB).transpose(1, 0, 2, 3).reshape(Z, 2 * chunk, NB),
        ],
        axis=1,
    )
    from_z = lax.all_to_all(to_z, "z", 0, 0)
    pieces = jnp.concatenate([from_z[0, :STEP], from_z[1, :2 * STEP]]).reshape(1, 3, STEP, NB)
    pieces = lax.all_to_all(
        jnp.broadcast_to(pieces, (X * Y * CORE, 3, STEP, NB)), PLANE, 0, 0
    )
    column = y * CORE + core
    raw = lax.dynamic_index_in_dim(from_z[:, 2 * STEP:], column, 0, keepdims=False)
    raw = raw.reshape(2, chunk, NB)

    inverse, lower, first_low = factor_leading(pieces)
    share = right_rows(raw, inverse, first_low)
    right = lax.all_to_all(
        jnp.broadcast_to(share[None], (X * Z, chunk, 2 * NB)), ("x", "z"), 0, 0
    ).reshape(CBL, NB, 2 * NB)
    return update(index, slab, left_first, left_second, right, inverse, lower, first_low)


def solution(mesh):
    inner = Mesh(mesh.devices.reshape(X, Z, Y, CORE), ("x", "z", "y", "core"))
    spec = P(None, ("x", "z"), None, ("y", "core"))
    return jax.shard_map(per_device, mesh=inner, in_specs=(spec,), out_specs=spec, check_vma=False)
```

```python
import functools
import jax
import jax.numpy as jnp
from jax import lax
from jax.experimental import pallas as pl
from jax.experimental.pallas import tpu as pltpu
from jax.sharding import Mesh
from jax.sharding import PartitionSpec as P

NB = 256
STEP = 8
HALF = 128
X, Z, Y, CORE = 4, 8, 4, 2
RBL, CBL = 6, 4
PART = RBL // 2
PLANE = ("x", "y", "core")


def times_transposed(left, right):
    return lax.dot_general(
        left, right, (((1,), (1,)), ((), ())), preferred_element_type=jnp.float32
    )


def lane_of(tile, lane):
    return jnp.broadcast_to(tile[:, lane:lane + 1], (STEP, HALF))


def row_of(tile, row):
    return jnp.broadcast_to(tile[row:row + 1, :], tile.shape)


def twice(value):
    return jnp.concatenate([value, value], axis=1)


def symmetric(value):
    rows = lax.broadcasted_iota(jnp.int32, (NB, NB), 0)
    cols = lax.broadcasted_iota(jnp.int32, (NB, NB), 1)
    return jnp.where(rows >= cols, value, value.T)


def factor(work, inverse_ref, upper_ref):
    lanes = lax.broadcasted_iota(jnp.int32, (STEP, NB), 1)
    rows = lax.broadcasted_iota(jnp.int32, (STEP, NB), 0)
    for step in range(NB // STEP):
        j = step * STEP
        half = j // HALF * HALF
        tile = work[j:j + STEP, :]
        diag = tile[:, half:half + HALF]
        cols = [lane_of(diag, j - half + k) for k in range(STEP)]
        left = [[row_of(cols[k], s) if k <= s else None for k in range(STEP)] for s in range(STEP)]
        low = [[None] * STEP for _ in range(STEP)]
        root = [None] * STEP
        inside = (lanes >= j) & (lanes < j + STEP)
        right = [
            jnp.where(inside, jnp.where(lanes == j + i, 1.0, 0.0), row_of(tile, i)) for i in range(STEP)
        ]
        solved = [None] * STEP
        for k in range(STEP):
            root[k] = lax.rsqrt(left[k][k])
            for s in range(k + 1, STEP):
                low[s][k] = left[s][k] * root[k]
            for s in range(k + 1, STEP):
                for m in range(k + 1, s + 1):
                    left[s][m] = left[s][m] - low[s][k] * low[m][k]
            solved[k] = right[k] * twice(root[k])
            for s in range(k + 1, STEP):
                right[s] = right[s] - twice(low[s][k]) * solved[k]
        weights = [None] * STEP
        for i in range(STEP - 1, -1, -1):
            total = solved[i]
            for s in range(i + 1, STEP):
                total = total - twice(low[s][i]) * weights[s]
            weights[i] = total * twice(root[i])
        for t in range(step + 1, NB // STEP):
            other = work[t * STEP:(t + 1) * STEP, :]
            side = other[:, half:half + HALF]
            total = jnp.where(inside, 0.0, other)
            for i in range(STEP):
                total = total - twice(lane_of(side, j - half + i)) * weights[i]
            work[t * STEP:(t + 1) * STEP, :] = total
        final = solved[0]
        for i in range(1, STEP):
            final = jnp.where(rows == i, solved[i], final)
        block = jnp.zeros((STEP, NB), jnp.float32)
        for i in range(STEP):
            for s in range(i, STEP):
                value = low[s][i] if s > i else left[i][i] * root[i]
                block = jnp.where((rows == i) & (lanes == j + s), twice(value), block)
        inverse_ref[j:j + STEP, :] = jnp.where(lanes < j + STEP, final, 0.0)
        upper_ref[j:j + STEP, :] = jnp.where(lanes >= j + STEP, final, block)


def split(value):
    high = value.astype(jnp.bfloat16)
    rest = value - high.astype(jnp.float32)
    middle = rest.astype(jnp.bfloat16)
    return high, middle, (rest - middle.astype(jnp.float32)).astype(jnp.bfloat16)


def times_table(value, table):
    high, middle, low = split(value)
    wide = jnp.concatenate([high, high, high, middle, middle, low], axis=1)
    return jnp.dot(wide, table, preferred_element_type=jnp.float32)


def leading_kernel(pieces, tables, lower, first_low, source, inverse, upper, work):
    for part in range(2):
        source[part] = pieces[:, 2 * part].reshape(NB, NB)

    @pl.loop(0, 2)
    def _(panel):
        work[...] = symmetric(source[panel])
        factor(work, inverse, upper)
        lower[panel] = upper[...].T
        high, middle, low = split(inverse[...].T)
        for place, term in enumerate([high, middle, low, high, middle, high]):
            tables[panel, place * NB:(place + 1) * NB, :] = term

        @pl.when(panel == 0)
        def _():
            rows = times_table(pieces[:, 1].reshape(NB, NB), tables[0]).astype(jnp.bfloat16)
            first_low[...] = rows.T
            source[1] = source[1] - times_transposed(rows, rows)


def factor_leading(pieces):
    whole = pl.BlockSpec(memory_space=pltpu.VMEM)
    square = pltpu.VMEM((NB, NB), jnp.float32)
    return pl.pallas_call(
        leading_kernel,
        out_shape=[
            jax.ShapeDtypeStruct((2, 6 * NB, NB), jnp.bfloat16),
            jax.ShapeDtypeStruct((2, NB, NB), jnp.float32),
            jax.ShapeDtypeStruct((NB, NB), jnp.bfloat16),
        ],
        in_specs=[whole],
        out_specs=[whole] * 3,
        scratch_shapes=[pltpu.VMEM((2, NB, NB), jnp.float32), square, square, square],
        compiler_params=pltpu.CompilerParams(vmem_limit_bytes=32 * 2**20),
        cost_estimate=pl.CostEstimate(flops=2**10, bytes_accessed=2**10, transcendentals=0),
        name="leading",
    )(pieces)


def panel_rows(raw_first, raw_second, tables, first_low):
    first = times_table(raw_first, tables[0])
    first_bf16 = first.astype(jnp.bfloat16)
    column = raw_second - jnp.dot(first_bf16, first_low[...], preferred_element_type=jnp.float32)
    second = times_table(column, tables[1])
    return first, first_bf16, second


def left_kernel(index, mine_low, other_low, mine_high, other_high, tables, lower, first_low, both, lead):
    step = pl.program_id(0)
    swap = index[1] % CORE == 1
    mine = jnp.concatenate([mine_low[0], mine_high[0]])
    other = jnp.concatenate([other_low[0], other_high[0]])
    raw_first = jnp.where(swap, other, mine)
    raw_second = jnp.where(swap, mine, other)
    first, first_bf16, second = panel_rows(raw_first, raw_second, tables, first_low)
    for part in range(2):
        row_block = (part * PART + step) * (X * Z) + index[0]
        rows = slice(part * NB, (part + 1) * NB)
        one, two, one_bf16 = first[rows], second[rows], first_bf16[rows]
        if part == 0:
            one = jnp.where(row_block == 0, lower[0], one)
            one_bf16 = one.astype(jnp.bfloat16)
            two = jnp.where(row_block == 1, lower[1], jnp.where(row_block == 0, 0.0, two))
        both[part, 0, :, :NB] = one_bf16
        both[part, 0, :, NB:] = two.astype(jnp.bfloat16)
        lead[part, 0] = jnp.where(swap, two, one)


def fixed(*shape):
    return pl.BlockSpec(shape, lambda b, _: (0,) * len(shape))


def by_row(*shape):
    return pl.BlockSpec((1,) + shape, lambda b, _: (b,) + (0,) * len(shape))


def left_rows(index, mine_low, other_low, mine_high, other_high, tables, lower, first_low):
    pair = lambda *shape: pl.BlockSpec((2, 1) + shape, lambda b, _: (0, b) + (0,) * len(shape))
    return pl.pallas_call(
        left_kernel,
        grid_spec=pltpu.PrefetchScalarGridSpec(
            num_scalar_prefetch=1,
            grid=(PART,),
            in_specs=[by_row(NB, NB)] * 4 + [fixed(2, 6 * NB, NB), fixed(2, NB, NB), fixed(NB, NB)],
            out_specs=[pair(NB, 2 * NB), pair(NB, NB)],
        ),
        out_shape=[
            jax.ShapeDtypeStruct((2, PART, NB, 2 * NB), jnp.bfloat16),
            jax.ShapeDtypeStruct((2, PART, NB, NB), jnp.float32),
        ],
        compiler_params=pltpu.CompilerParams(vmem_limit_bytes=32 * 2**20),
        cost_estimate=pl.CostEstimate(flops=2**10, bytes_accessed=2**10, transcendentals=0),
        name="left_rows",
    )(index, mine_low, other_low, mine_high, other_high, tables, lower, first_low)


def update_kernel(index, slab, both, lead, raw, tables, first_low, out, right):
    row_block = pl.program_id(0) * (X * Z) + index[0]
    col_index = index[1]

    @pl.when(pl.program_id(0) == 0)
    def _():
        for m in range(CBL):
            raw_first = raw[m * Z:(m + 1) * Z, 0].reshape(NB, NB)
            raw_second = raw[m * Z:(m + 1) * Z, 1].reshape(NB, NB)
            _, first_bf16, second = panel_rows(raw_first, raw_second, tables, first_low)
            columns = slice(m * NB, (m + 1) * NB)
            right[:NB, columns] = first_bf16.T
            right[NB:, columns] = second.astype(jnp.bfloat16).T

    change = jnp.dot(both[0, 0], right[...], preferred_element_type=jnp.float32)
    for m in range(CBL):
        live = (row_block >= 2) & (m * (Y * CORE) + col_index >= 2)
        value = slab[0, :, m, :] - jnp.where(live, change[:, m * NB:(m + 1) * NB], 0.0)
        if m == 0:
            value = jnp.where(col_index < 2, lead[0, 0], value)
        out[0, :, m, :] = value


def update(index, slab, both, lead, raw, tables, first_low):
    part = lambda *shape: pl.BlockSpec(
        (1, 1) + shape, lambda b, _: (b // PART, b % PART) + (0,) * len(shape)
    )
    return pl.pallas_call(
        update_kernel,
        grid_spec=pltpu.PrefetchScalarGridSpec(
            num_scalar_prefetch=1,
            grid=(RBL,),
            in_specs=[
                by_row(NB, CBL, NB), part(NB, 2 * NB), part(NB, NB),
                fixed(X * Z, 2, NB // Z, NB), fixed(2, 6 * NB, NB), fixed(NB, NB),
            ],
            out_specs=by_row(NB, CBL, NB),
            scratch_shapes=[pltpu.VMEM((2 * NB, CBL * NB), jnp.bfloat16)],
        ),
        out_shape=jax.ShapeDtypeStruct(slab.shape, jnp.float32),
        compiler_params=pltpu.CompilerParams(vmem_limit_bytes=40 * 2**20),
        cost_estimate=pl.CostEstimate(flops=2**10, bytes_accessed=2**10, transcendentals=0),
        name="update",
    )(index, slab, both, lead, raw, tables, first_low)


def tie(value, *others):
    return lax.optimization_barrier((value,) + others)[0]


def per_device(slab):
    x, z = lax.axis_index("x"), lax.axis_index("z")
    y, core = lax.axis_index("y"), lax.axis_index("core")
    column = y * CORE + core
    index = jnp.stack([x * Z + z, column]).astype(jnp.int32)
    top = slab[0, :, 0, :]
    own_low = slab[1:PART, :, 0, :]
    own_high = slab[PART:, :, 0, :]
    chunk = NB // Z

    def place(k):
        pairs = [(zz * Y * CORE + k, zz * Y * CORE + zz) for zz in range(Z)]
        return lax.ppermute(top, ("z", "y", "core"), pairs)

    scattered = lax.all_to_all(top.reshape(X * Y * CORE, STEP, NB), PLANE, 0, 0)[:2]
    one_top = lax.ppermute(top, "y", [(0, 1)])
    three_top = lax.ppermute(top, "y", [(0, 3)])
    scattered = tie(scattered, own_low, own_high, one_top, three_top)
    placed = jnp.stack([place(0), place(1)])
    to_z = jnp.concatenate(
        [
            jnp.broadcast_to(scattered.reshape(1, 2 * STEP, NB), (Z, 2 * STEP, NB)),
            placed.reshape(2, Z, chunk, NB).transpose(1, 0, 2, 3).reshape(Z, 2 * chunk, NB),
        ],
        axis=1,
    )
    one_low = lax.ppermute(own_low, "y", [(0, 1)])
    three_low = lax.ppermute(own_low, "y", [(0, 3)])
    join = lambda first, rest: jnp.concatenate([first[None], rest])
    from_z = lax.all_to_all(to_z, "z", 0, 0)
    from_z = tie(from_z, one_low, three_low)
    own_low, one_low, three_low = join(top, own_low), join(one_top, one_low), join(three_top, three_low)
    pieces = jnp.concatenate([from_z[0, :STEP], from_z[1, :2 * STEP]]).reshape(1, 3, STEP, NB)
    one_high = lax.ppermute(own_high, "y", [(0, 1)])
    three_high = lax.ppermute(own_high, "y", [(0, 3)])
    two_low = lax.ppermute(one_low, "y", [(1, 2)])
    pieces = lax.all_to_all(
        jnp.broadcast_to(pieces, (X * Y * CORE, 3, STEP, NB)), PLANE, 0, 0
    )
    pieces = tie(pieces, one_high, three_high)
    two_high = lax.ppermute(three_high, "y", [(3, 2)])
    raw = lax.dynamic_index_in_dim(from_z[:, 2 * STEP:], column, 0).reshape(1, 2, chunk, NB)
    raw = jnp.broadcast_to(raw, (X * Z, 2, chunk, NB))
    raw = lax.all_to_all(tie(raw, pieces, one_high, three_high), ("x", "z"), 0, 0)

    tables, lower, first_low = factor_leading(pieces)

    def panel(own, one, two, three):
        mine = jnp.where(y == 0, own, jnp.where(y == 1, one, jnp.where(y == 3, three, two)))
        return mine, lax.ppermute(mine, "core", [(0, 1), (1, 0)])

    low = panel(own_low, one_low, tie(two_low, tables), three_low)
    high = panel(own_high, one_high, tie(two_high, tables), three_high)
    both, lead = left_rows(index, *low, *high, tables, lower, first_low)
    return update(index, slab, both, lead, raw, tables, first_low)


def solution(mesh):
    inner = Mesh(mesh.devices.reshape(X, Z, Y, CORE), ("x", "z", "y", "core"))
    spec = P(None, ("x", "z"), None, ("y", "core"))
    return jax.shard_map(per_device, mesh=inner, in_specs=(spec,), out_specs=spec, check_vma=False)
```

```python
import functools
import jax
import jax.numpy as jnp
from jax import lax
from jax.experimental import pallas as pl
from jax.experimental.pallas import tpu as pltpu
from jax.sharding import Mesh
from jax.sharding import PartitionSpec as P

NB = 256
STEP = 8
HALF = 128
X, Z, Y, CORE = 4, 8, 4, 2
RBL, CBL = 6, 4
PART = RBL // 2
PLANE = ("x", "y", "core")


def times_transposed(left, right):
    return lax.dot_general(
        left, right, (((1,), (1,)), ((), ())), preferred_element_type=jnp.float32
    )


def lane_of(tile, lane):
    return jnp.broadcast_to(tile[:, lane:lane + 1], (STEP, HALF))


def row_of(tile, row):
    return jnp.broadcast_to(tile[row:row + 1, :], tile.shape)


def twice(value):
    return jnp.concatenate([value, value], axis=1)


def symmetric(value):
    rows = lax.broadcasted_iota(jnp.int32, (NB, NB), 0)
    cols = lax.broadcasted_iota(jnp.int32, (NB, NB), 1)
    return jnp.where(rows >= cols, value, value.T)


def factor(work, inverse_ref, upper_ref):
    lanes = lax.broadcasted_iota(jnp.int32, (STEP, NB), 1)
    rows = lax.broadcasted_iota(jnp.int32, (STEP, NB), 0)
    for step in range(NB // STEP):
        j = step * STEP
        half = j // HALF * HALF
        tile = work[j:j + STEP, :]
        diag = tile[:, half:half + HALF]
        cols = [lane_of(diag, j - half + k) for k in range(STEP)]
        left = [[row_of(cols[k], s) if k <= s else None for k in range(STEP)] for s in range(STEP)]
        low = [[None] * STEP for _ in range(STEP)]
        root = [None] * STEP
        inside = (lanes >= j) & (lanes < j + STEP)
        right = [
            jnp.where(inside, jnp.where(lanes == j + i, 1.0, 0.0), row_of(tile, i)) for i in range(STEP)
        ]
        solved = [None] * STEP
        for k in range(STEP):
            root[k] = lax.rsqrt(left[k][k])
            for s in range(k + 1, STEP):
                low[s][k] = left[s][k] * root[k]
            for s in range(k + 1, STEP):
                for m in range(k + 1, s + 1):
                    left[s][m] = left[s][m] - low[s][k] * low[m][k]
            solved[k] = right[k] * twice(root[k])
            for s in range(k + 1, STEP):
                right[s] = right[s] - twice(low[s][k]) * solved[k]
        if step + 1 < NB // STEP:
            rest = work[j + STEP:j + 2 * STEP, :]
            side = rest[:, half:half + HALF]
            ahead = [lane_of(side, j - half + k) for k in range(STEP)]
            total = jnp.where(inside, 0.0, rest)
            for k in range(STEP):
                ahead[k] = ahead[k] * root[k]
                for s in range(k + 1, STEP):
                    ahead[s] = ahead[s] - ahead[k] * low[s][k]
                total = total - twice(ahead[k]) * solved[k]
            work[j + STEP:j + 2 * STEP, :] = total
        weights = [None] * STEP
        for i in range(STEP - 1, -1, -1):
            total = solved[i]
            for s in range(i + 1, STEP):
                total = total - twice(low[s][i]) * weights[s]
            weights[i] = total * twice(root[i])
        for t in range(step + 2, NB // STEP):
            other = work[t * STEP:(t + 1) * STEP, :]
            side = other[:, half:half + HALF]
            total = jnp.where(inside, 0.0, other)
            for i in range(STEP):
                total = total - twice(lane_of(side, j - half + i)) * weights[i]
            work[t * STEP:(t + 1) * STEP, :] = total
        final = solved[0]
        for i in range(1, STEP):
            final = jnp.where(rows == i, solved[i], final)
        block = jnp.zeros((STEP, NB), jnp.float32)
        for i in range(STEP):
            for s in range(i, STEP):
                value = low[s][i] if s > i else left[i][i] * root[i]
                block = jnp.where((rows == i) & (lanes == j + s), twice(value), block)
        inverse_ref[j:j + STEP, :] = jnp.where(lanes < j + STEP, final, 0.0)
        upper_ref[j:j + STEP, :] = jnp.where(lanes >= j + STEP, final, block)


def split(value):
    high = value.astype(jnp.bfloat16)
    rest = value - high.astype(jnp.float32)
    middle = rest.astype(jnp.bfloat16)
    return high, middle, (rest - middle.astype(jnp.float32)).astype(jnp.bfloat16)


def times_table(value, table):
    high, middle, low = split(value)
    wide = jnp.concatenate([high, high, high, middle, middle, low], axis=1)
    return jnp.dot(wide, table, preferred_element_type=jnp.float32)


def leading_kernel(pieces, tables, lower, first_low, source, inverse, upper, work):
    for part in range(2):
        source[part] = pieces[:, 2 * part].reshape(NB, NB)

    @pl.loop(0, 2)
    def _(panel):
        work[...] = symmetric(source[panel])
        factor(work, inverse, upper)
        lower[panel] = upper[...].T
        high, middle, low = split(inverse[...].T)
        for place, term in enumerate([high, middle, low, high, middle, high]):
            tables[panel, place * NB:(place + 1) * NB, :] = term

        @pl.when(panel == 0)
        def _():
            rows = times_table(pieces[:, 1].reshape(NB, NB), tables[0]).astype(jnp.bfloat16)
            first_low[...] = rows.T
            source[1] = source[1] - times_transposed(rows, rows)


def factor_leading(pieces):
    whole = pl.BlockSpec(memory_space=pltpu.VMEM)
    square = pltpu.VMEM((NB, NB), jnp.float32)
    return pl.pallas_call(
        leading_kernel,
        out_shape=[
            jax.ShapeDtypeStruct((2, 6 * NB, NB), jnp.bfloat16),
            pltpu.HBM((2, NB, NB), jnp.float32),
            jax.ShapeDtypeStruct((NB, NB), jnp.bfloat16),
        ],
        in_specs=[whole],
        out_specs=[whole] * 3,
        scratch_shapes=[pltpu.VMEM((2, NB, NB), jnp.float32), square, square, square],
        compiler_params=pltpu.CompilerParams(vmem_limit_bytes=16 * 2**20),
        cost_estimate=pl.CostEstimate(flops=2**10, bytes_accessed=2**10, transcendentals=0),
        name="leading",
    )(pieces)


def panel_rows(raw_first, raw_second, tables, first_low):
    first = times_table(raw_first, tables[0])
    first_bf16 = first.astype(jnp.bfloat16)
    column = raw_second - jnp.dot(first_bf16, first_low[...], preferred_element_type=jnp.float32)
    second = times_table(column, tables[1])
    return first, first_bf16, second


def left_kernel(index, mine, other, tables, lower, first_low, both, keep, give):
    row_block = (index[2] * PART + pl.program_id(0)) * (X * Z) + index[0]
    swap = index[2] == 1
    raw_first = jnp.where(swap, other[0], mine[0])
    raw_second = jnp.where(swap, mine[0], other[0])
    first, first_bf16, second = panel_rows(raw_first, raw_second, tables, first_low)
    first = jnp.where(row_block == 0, lower[0], first)
    second = jnp.where(row_block == 1, lower[1], jnp.where(row_block == 0, 0.0, second))
    both[0, :, :NB] = first.astype(jnp.bfloat16)
    both[0, :, NB:] = second.astype(jnp.bfloat16)
    keep[0] = jnp.where(swap, second, first)
    give[0] = jnp.where(swap, first, second)


def fixed(*shape):
    return pl.BlockSpec(shape, lambda b, _: (0,) * len(shape))


def by_row(*shape):
    return pl.BlockSpec((1,) + shape, lambda b, _: (b,) + (0,) * len(shape))


def left_rows(index, mine, other, tables, lower, first_low):
    panel = pltpu.HBM((PART, NB, NB), jnp.float32)
    return pl.pallas_call(
        left_kernel,
        grid_spec=pltpu.PrefetchScalarGridSpec(
            num_scalar_prefetch=1,
            grid=(PART,),
            in_specs=[by_row(NB, NB)] * 2 + [fixed(2, 6 * NB, NB), fixed(2, NB, NB), fixed(NB, NB)],
            out_specs=[by_row(NB, 2 * NB), by_row(NB, NB), by_row(NB, NB)],
        ),
        out_shape=[pltpu.HBM((PART, NB, 2 * NB), jnp.bfloat16), panel, panel],
        compiler_params=pltpu.CompilerParams(vmem_limit_bytes=20 * 2**20),
        cost_estimate=pl.CostEstimate(flops=2**10, bytes_accessed=2**10, transcendentals=0),
        name="left_rows",
    )(index, mine, other, tables, in_hbm(lower), first_low)


def right_kernel(raw, tables, first_low, out):
    raw_first, raw_second = (raw[:, part].reshape(NB, NB) for part in range(2))
    _, first_bf16, second = panel_rows(raw_first, raw_second, tables, first_low)
    second_bf16 = second.astype(jnp.bfloat16)
    for device in range(X):
        out[device, :, :NB] = first_bf16
        out[device, :, NB:] = second_bf16


def right_rows(raw, tables, first_low):
    whole = pl.BlockSpec(memory_space=pltpu.VMEM)
    return pl.pallas_call(
        right_kernel,
        out_shape=pltpu.HBM((X, NB, 2 * NB), jnp.bfloat16),
        in_specs=[whole] * 3,
        out_specs=whole,
        compiler_params=pltpu.CompilerParams(vmem_limit_bytes=16 * 2**20),
        cost_estimate=pl.CostEstimate(flops=2**10, bytes_accessed=2**10, transcendentals=0),
        name="right_rows",
    )(raw, tables, first_low)


def update_kernel(index, slab, both_mine, both_other, lead_mine, lead_other, right, out):
    col_index = index[1]
    for part in range(2):
        own = index[2] == part
        row_block = (part * PART + pl.program_id(0)) * (X * Z) + index[0]
        both = jnp.where(own, both_mine[0], both_other[0])
        for m in range(CBL):
            change = times_transposed(both, right[m])
            live = (row_block >= 2) & (m * (Y * CORE) + col_index >= 2)
            value = slab[part, 0, :, m, :] - jnp.where(live, change, 0.0)
            if m == 0:
                lead = jnp.where(own, lead_mine[0], lead_other[0])
                value = jnp.where(col_index < 2, lead, value)
            out[part, 0, :, m, :] = value


def update(index, slab, both_mine, both_other, lead_mine, lead_other, right):
    halves = (2, PART) + slab.shape[1:]
    place = pl.BlockSpec((2, 1, NB, CBL, NB), lambda s, _: (0, s, 0, 0, 0))
    return pl.pallas_call(
        update_kernel,
        grid_spec=pltpu.PrefetchScalarGridSpec(
            num_scalar_prefetch=1,
            grid=(PART,),
            in_specs=[
                place, by_row(NB, 2 * NB), by_row(NB, 2 * NB), by_row(NB, NB), by_row(NB, NB),
                fixed(CBL, NB, 2 * NB),
            ],
            out_specs=place,
        ),
        out_shape=jax.ShapeDtypeStruct(halves, jnp.float32),
        compiler_params=pltpu.CompilerParams(vmem_limit_bytes=30 * 2**20),
        cost_estimate=pl.CostEstimate(flops=2**10, bytes_accessed=2**10, transcendentals=0),
        name="update",
    )(
        index, in_hbm(slab.reshape(halves)), in_hbm(both_mine), both_other, in_hbm(lead_mine),
        lead_other, right,
    ).reshape(slab.shape)


def in_hbm(value):
    return pltpu.with_memory_space_constraint(value, pltpu.HBM)


def tie(value, *others):
    return lax.optimization_barrier((value,) + others)[0]


def per_device(slab):
    x, z = lax.axis_index("x"), lax.axis_index("z")
    y, core = lax.axis_index("y"), lax.axis_index("core")
    column = y * CORE + core
    index = jnp.stack([x * Z + z, column, core]).astype(jnp.int32)
    top = slab[0, :, 0, :]
    chunk = NB // Z
    swapped = [(0, 1), (1, 0)]

    def half(which):
        rows = lax.dynamic_slice(slab, (which * PART, 0, 0, 0), (PART, NB, 1, NB))
        return rows.reshape(PART, NB, NB)

    mine_zero = half(core)
    other_zero = lax.ppermute(half(1 - core), "core", swapped)

    def place(k):
        pairs = [(zz * Y * CORE + k, zz * Y * CORE + zz) for zz in range(Z)]
        return lax.ppermute(top, ("z", "y", "core"), pairs)

    scattered = lax.all_to_all(top.reshape(X * Y * CORE, STEP, NB), PLANE, 0, 0)[:2]
    scattered = tie(scattered, mine_zero)
    placed = jnp.stack([place(0), place(1)])
    to_z = jnp.concatenate(
        [
            jnp.broadcast_to(scattered.reshape(1, 2 * STEP, NB), (Z, 2 * STEP, NB)),
            placed.reshape(2, Z, chunk, NB).transpose(1, 0, 2, 3).reshape(Z, 2 * chunk, NB),
        ],
        axis=1,
    )
    mine_one = lax.ppermute(mine_zero, "y", [(0, 1)])
    mine_three = lax.ppermute(mine_zero, "y", [(0, 3)])
    from_z = lax.all_to_all(to_z, "z", 0, 0)
    from_z = tie(from_z, mine_one, mine_three, other_zero)
    pieces = jnp.concatenate([from_z[0, :STEP], from_z[1, :2 * STEP]]).reshape(1, 3, STEP, NB)
    other_one = lax.ppermute(other_zero, "y", [(0, 1)])
    other_three = lax.ppermute(other_zero, "y", [(0, 3)])
    mine_two = lax.ppermute(mine_one, "y", [(1, 2)])
    pieces = lax.all_to_all(
        jnp.broadcast_to(pieces, (X * Y * CORE, 3, STEP, NB)), PLANE, 0, 0
    )
    pieces = tie(pieces, other_one, other_three)
    other_two = lax.ppermute(other_three, "y", [(3, 2)])
    raw = lax.dynamic_index_in_dim(from_z[:, 2 * STEP:], column, 0).reshape(1, 2, chunk, NB)
    raw = jnp.broadcast_to(raw, (Z, 2, chunk, NB))
    raw = lax.all_to_all(tie(raw, pieces, other_one, other_three, mine_two), "z", 0, 0)

    tables, lower, first_low = factor_leading(pieces)

    share = right_rows(raw, tables, first_low)
    right = lax.all_to_all(share, "x", 0, 0)

    def select(zero, one, two, three):
        return jnp.where(y == 0, zero, jnp.where(y == 1, one, jnp.where(y == 3, three, two)))

    mine = select(mine_zero, mine_one, tie(mine_two, share), mine_three)
    other = select(other_zero, other_one, tie(other_two, share), other_three)
    both, keep, give = left_rows(index, mine, other, tables, lower, first_low)
    both_other = lax.ppermute(both, "core", swapped)
    lead_other = lax.ppermute(give, ("y", "core"), swapped)
    return update(index, slab, both, both_other, keep, lead_other, right)


def solution(mesh):
    inner = Mesh(mesh.devices.reshape(X, Z, Y, CORE), ("x", "z", "y", "core"))
    spec = P(None, ("x", "z"), None, ("y", "core"))
    return jax.shard_map(per_device, mesh=inner, in_specs=(spec,), out_specs=spec, check_vma=False)
```

```python
import functools
import jax
import jax.numpy as jnp
from jax import lax
from jax.experimental import pallas as pl
from jax.experimental.pallas import tpu as pltpu
from jax.sharding import Mesh
from jax.sharding import PartitionSpec as P

NB = 256
STEP = 8
HALF = 128
X, Z, Y, CORE = 4, 8, 4, 2
RBL, CBL = 6, 4
PART = RBL // 2
PLANE = ("x", "y", "core")


def times_transposed(left, right):
    return lax.dot_general(
        left, right, (((1,), (1,)), ((), ())), preferred_element_type=jnp.float32
    )


def lane_of(tile, lane):
    return jnp.broadcast_to(tile[:, lane:lane + 1], (STEP, HALF))


def row_of(tile, row):
    return jnp.broadcast_to(tile[row:row + 1, :], tile.shape)


def symmetric(value):
    rows = lax.broadcasted_iota(jnp.int32, value.shape, 0)
    cols = lax.broadcasted_iota(jnp.int32, value.shape, 1)
    return jnp.where(rows >= cols, value, value.T)


def factor(work, inverse_ref, upper_ref):
    lanes = lax.broadcasted_iota(jnp.int32, (STEP, HALF), 1)
    rows = lax.broadcasted_iota(jnp.int32, (STEP, HALF), 0)
    for step in range(HALF // STEP):
        j = step * STEP
        tile = work[j:j + STEP, :]
        cols = [lane_of(tile, j + k) for k in range(STEP)]
        left = [[row_of(cols[k], s) if k <= s else None for k in range(STEP)] for s in range(STEP)]
        low = [[None] * STEP for _ in range(STEP)]
        root = [None] * STEP
        inside = (lanes >= j) & (lanes < j + STEP)
        right = [
            jnp.where(inside, jnp.where(lanes == j + i, 1.0, 0.0), row_of(tile, i)) for i in range(STEP)
        ]
        solved = [None] * STEP
        for k in range(STEP):
            root[k] = lax.rsqrt(left[k][k])
            for s in range(k + 1, STEP):
                low[s][k] = left[s][k] * root[k]
            for s in range(k + 1, STEP):
                for m in range(k + 1, s + 1):
                    left[s][m] = left[s][m] - low[s][k] * low[m][k]
            solved[k] = right[k] * root[k]
            for s in range(k + 1, STEP):
                right[s] = right[s] - low[s][k] * solved[k]
        if step + 1 < HALF // STEP:
            rest = work[j + STEP:j + 2 * STEP, :]
            ahead = [lane_of(rest, j + k) for k in range(STEP)]
            total = jnp.where(inside, 0.0, rest)
            for k in range(STEP):
                ahead[k] = ahead[k] * root[k]
                for s in range(k + 1, STEP):
                    ahead[s] = ahead[s] - ahead[k] * low[s][k]
                total = total - ahead[k] * solved[k]
            work[j + STEP:j + 2 * STEP, :] = total
        weights = [None] * STEP
        for i in range(STEP - 1, -1, -1):
            total = solved[i]
            for s in range(i + 1, STEP):
                total = total - low[s][i] * weights[s]
            weights[i] = total * root[i]
        for t in range(step + 2, HALF // STEP):
            other = work[t * STEP:(t + 1) * STEP, :]
            total = jnp.where(inside, 0.0, other)
            for i in range(STEP):
                total = total - lane_of(other, j + i) * weights[i]
            work[t * STEP:(t + 1) * STEP, :] = total
        final = solved[0]
        for i in range(1, STEP):
            final = jnp.where(rows == i, solved[i], final)
        block = jnp.zeros((STEP, HALF), jnp.float32)
        for i in range(STEP):
            for s in range(i, STEP):
                value = low[s][i] if s > i else left[i][i] * root[i]
                block = jnp.where((rows == i) & (lanes == j + s), value, block)
        inverse_ref[j:j + STEP, :] = jnp.where(lanes < j + STEP, final, 0.0)
        upper_ref[j:j + STEP, :] = jnp.where(lanes >= j + STEP, final, block)


def split(value):
    high = value.astype(jnp.bfloat16)
    rest = value - high.astype(jnp.float32)
    middle = rest.astype(jnp.bfloat16)
    return high, middle, (rest - middle.astype(jnp.float32)).astype(jnp.bfloat16)


def times_table(value, table):
    high, middle, low = split(value)
    wide = jnp.concatenate([high, high, high, middle, middle, low], axis=1)
    return jnp.dot(wide, table, preferred_element_type=jnp.float32)


def table_of(value):
    high, middle, low = split(value)
    return jnp.concatenate([high, middle, low, high, middle, high])


def leading_kernel(pieces, tables, lower, first_low, source, first_inverse, below, inverse, upper, work):
    for part in range(2):
        source[part] = pieces[:, 2 * part].reshape(NB, NB)
    work[...] = symmetric(source[0, :HALF, :HALF])
    zeros = jnp.zeros((HALF, HALF), jnp.float32)

    @pl.loop(0, 4)
    def _(part):
        panel = part // 2
        factor(work, inverse, upper)

        @pl.when(part % 2 == 0)
        def _():
            first_inverse[...] = inverse[...]
            side = times_table(source[panel, HALF:, :HALF], table_of(inverse[...].T))
            below[...] = side
            work[...] = symmetric(source[panel, HALF:, HALF:] - times_table(side, table_of(side.T)))
            lower[panel, :HALF, :HALF] = upper[...].T
            lower[panel, :HALF, HALF:] = zeros
            lower[panel, HALF:, :HALF] = side

        @pl.when(part % 2 == 1)
        def _():
            corner = times_table(below[...], table_of(first_inverse[...]))
            corner = -times_table(inverse[...], table_of(corner))
            top = jnp.concatenate([first_inverse[...].T, corner.T], axis=1)
            bottom = jnp.concatenate([zeros, inverse[...].T], axis=1)
            tables[panel] = table_of(jnp.concatenate([top, bottom]))
            lower[panel, HALF:, HALF:] = upper[...].T

        @pl.when(part == 1)
        def _():
            rows = times_table(pieces[:, 1].reshape(NB, NB), tables[0]).astype(jnp.bfloat16)
            first_low[...] = rows.T
            source[1] = source[1] - times_transposed(rows, rows)
            work[...] = symmetric(source[1, :HALF, :HALF])


def factor_leading(pieces):
    whole = pl.BlockSpec(memory_space=pltpu.VMEM)
    square = pltpu.VMEM((HALF, HALF), jnp.float32)
    return pl.pallas_call(
        leading_kernel,
        out_shape=[
            jax.ShapeDtypeStruct((2, 6 * NB, NB), jnp.bfloat16),
            pltpu.HBM((2, NB, NB), jnp.float32),
            jax.ShapeDtypeStruct((NB, NB), jnp.bfloat16),
        ],
        in_specs=[whole],
        out_specs=[whole] * 3,
        scratch_shapes=[pltpu.VMEM((2, NB, NB), jnp.float32)] + [square] * 5,
        compiler_params=pltpu.CompilerParams(vmem_limit_bytes=16 * 2**20),
        cost_estimate=pl.CostEstimate(flops=2**10, bytes_accessed=2**10, transcendentals=0),
        name="leading",
    )(pieces)


def panel_rows(raw_first, raw_second, tables, first_low):
    first = times_table(raw_first, tables[0])
    first_bf16 = first.astype(jnp.bfloat16)
    column = raw_second - jnp.dot(first_bf16, first_low[...], preferred_element_type=jnp.float32)
    second = times_table(column, tables[1])
    return first, first_bf16, second


def left_kernel(index, mine, other, tables, lower, first_low, both, keep, give):
    row_block = (index[2] * PART + pl.program_id(0)) * (X * Z) + index[0]
    swap = index[2] == 1
    raw_first = jnp.where(swap, other[0], mine[0])
    raw_second = jnp.where(swap, mine[0], other[0])
    first, first_bf16, second = panel_rows(raw_first, raw_second, tables, first_low)
    first = jnp.where(row_block == 0, lower[0], first)
    second = jnp.where(row_block == 1, lower[1], jnp.where(row_block == 0, 0.0, second))
    both[0, :, :NB] = first.astype(jnp.bfloat16)
    both[0, :, NB:] = second.astype(jnp.bfloat16)
    keep[0] = jnp.where(swap, second, first)
    give[0] = jnp.where(swap, first, second)


def fixed(*shape):
    return pl.BlockSpec(shape, lambda b, _: (0,) * len(shape))


def by_row(*shape):
    return pl.BlockSpec((1,) + shape, lambda b, _: (b,) + (0,) * len(shape))


def left_rows(index, mine, other, tables, lower, first_low):
    panel = pltpu.HBM((PART, NB, NB), jnp.float32)
    return pl.pallas_call(
        left_kernel,
        grid_spec=pltpu.PrefetchScalarGridSpec(
            num_scalar_prefetch=1,
            grid=(PART,),
            in_specs=[by_row(NB, NB)] * 2 + [fixed(2, 6 * NB, NB), fixed(2, NB, NB), fixed(NB, NB)],
            out_specs=[by_row(NB, 2 * NB), by_row(NB, NB), by_row(NB, NB)],
        ),
        out_shape=[pltpu.HBM((PART, NB, 2 * NB), jnp.bfloat16), panel, panel],
        compiler_params=pltpu.CompilerParams(vmem_limit_bytes=20 * 2**20),
        cost_estimate=pl.CostEstimate(flops=2**10, bytes_accessed=2**10, transcendentals=0),
        name="left_rows",
    )(index, mine, other, tables, in_hbm(lower), first_low)


def right_kernel(raw, tables, first_low, out):
    raw_first, raw_second = (raw[:, part].reshape(NB, NB) for part in range(2))
    _, first_bf16, second = panel_rows(raw_first, raw_second, tables, first_low)
    second_bf16 = second.astype(jnp.bfloat16)
    for device in range(X):
        out[device, :, :NB] = first_bf16
        out[device, :, NB:] = second_bf16


def right_rows(raw, tables, first_low):
    whole = pl.BlockSpec(memory_space=pltpu.VMEM)
    return pl.pallas_call(
        right_kernel,
        out_shape=pltpu.HBM((X, NB, 2 * NB), jnp.bfloat16),
        in_specs=[whole] * 3,
        out_specs=whole,
        compiler_params=pltpu.CompilerParams(vmem_limit_bytes=16 * 2**20),
        cost_estimate=pl.CostEstimate(flops=2**10, bytes_accessed=2**10, transcendentals=0),
        name="right_rows",
    )(raw, tables, first_low)


def update_kernel(index, slab, both_mine, both_other, lead_mine, lead_other, right, out):
    col_index = index[1]
    for part in range(2):
        own = index[2] == part
        row_block = (part * PART + pl.program_id(0)) * (X * Z) + index[0]
        both = jnp.where(own, both_mine[0], both_other[0])
        for m in range(CBL):
            change = times_transposed(both, right[m])
            live = (row_block >= 2) & (m * (Y * CORE) + col_index >= 2)
            value = slab[part, 0, :, m, :] - jnp.where(live, change, 0.0)
            if m == 0:
                lead = jnp.where(own, lead_mine[0], lead_other[0])
                value = jnp.where(col_index < 2, lead, value)
            out[part, 0, :, m, :] = value


def update(index, slab, both_mine, both_other, lead_mine, lead_other, right):
    halves = (2, PART) + slab.shape[1:]
    place = pl.BlockSpec((2, 1, NB, CBL, NB), lambda s, _: (0, s, 0, 0, 0))
    return pl.pallas_call(
        update_kernel,
        grid_spec=pltpu.PrefetchScalarGridSpec(
            num_scalar_prefetch=1,
            grid=(PART,),
            in_specs=[
                place, by_row(NB, 2 * NB), by_row(NB, 2 * NB), by_row(NB, NB), by_row(NB, NB),
                fixed(CBL, NB, 2 * NB),
            ],
            out_specs=place,
        ),
        out_shape=jax.ShapeDtypeStruct(halves, jnp.float32),
        compiler_params=pltpu.CompilerParams(vmem_limit_bytes=30 * 2**20),
        cost_estimate=pl.CostEstimate(flops=2**10, bytes_accessed=2**10, transcendentals=0),
        name="update",
    )(
        index, in_hbm(slab.reshape(halves)), in_hbm(both_mine), both_other, in_hbm(lead_mine),
        lead_other, right,
    ).reshape(slab.shape)


def in_hbm(value):
    return pltpu.with_memory_space_constraint(value, pltpu.HBM)


def tie(value, *others):
    return lax.optimization_barrier((value,) + others)[0]


def per_device(slab):
    x, z = lax.axis_index("x"), lax.axis_index("z")
    y, core = lax.axis_index("y"), lax.axis_index("core")
    column = y * CORE + core
    index = jnp.stack([x * Z + z, column, core]).astype(jnp.int32)
    top = slab[0, :, 0, :]
    chunk = NB // Z
    swapped = [(0, 1), (1, 0)]

    def half(which):
        rows = lax.dynamic_slice(slab, (which * PART, 0, 0, 0), (PART, NB, 1, NB))
        return rows.reshape(PART, NB, NB)

    mine_zero = half(core)
    other_zero = lax.ppermute(half(1 - core), "core", swapped)

    def place(k):
        pairs = [(zz * Y * CORE + k, zz * Y * CORE + zz) for zz in range(Z)]
        return lax.ppermute(top, ("z", "y", "core"), pairs)

    scattered = lax.all_to_all(top.reshape(X * Y * CORE, STEP, NB), PLANE, 0, 0)[:2]
    scattered = tie(scattered, mine_zero)
    placed = jnp.stack([place(0), place(1)])
    to_z = jnp.concatenate(
        [
            jnp.broadcast_to(scattered.reshape(1, 2 * STEP, NB), (Z, 2 * STEP, NB)),
            placed.reshape(2, Z, chunk, NB).transpose(1, 0, 2, 3).reshape(Z, 2 * chunk, NB),
        ],
        axis=1,
    )
    mine_one = lax.ppermute(mine_zero, "y", [(0, 1)])
    mine_three = lax.ppermute(mine_zero, "y", [(0, 3)])
    from_z = lax.all_to_all(to_z, "z", 0, 0)
    from_z = tie(from_z, mine_one, mine_three, other_zero)
    pieces = jnp.concatenate([from_z[0, :STEP], from_z[1, :2 * STEP]]).reshape(1, 3, STEP, NB)
    other_one = lax.ppermute(other_zero, "y", [(0, 1)])
    other_three = lax.ppermute(other_zero, "y", [(0, 3)])
    mine_two = lax.ppermute(mine_one, "y", [(1, 2)])
    pieces = lax.all_to_all(
        jnp.broadcast_to(pieces, (X * Y * CORE, 3, STEP, NB)), PLANE, 0, 0
    )
    pieces = tie(pieces, other_one, other_three)
    other_two = lax.ppermute(other_three, "y", [(3, 2)])
    raw = lax.dynamic_index_in_dim(from_z[:, 2 * STEP:], column, 0).reshape(1, 2, chunk, NB)
    raw = jnp.broadcast_to(raw, (Z, 2, chunk, NB))
    raw = lax.all_to_all(tie(raw, pieces, other_one, other_three, mine_two), "z", 0, 0)

    tables, lower, first_low = factor_leading(pieces)

    share = right_rows(raw, tables, first_low)
    right = lax.all_to_all(share, "x", 0, 0)

    def select(zero, one, two, three):
        return jnp.where(y == 0, zero, jnp.where(y == 1, one, jnp.where(y == 3, three, two)))

    mine = select(mine_zero, mine_one, tie(mine_two, share), mine_three)
    other = select(other_zero, other_one, tie(other_two, share), other_three)
    both, keep, give = left_rows(index, mine, other, tables, lower, first_low)
    both_other = lax.ppermute(both, "core", swapped)
    lead_other = lax.ppermute(give, ("y", "core"), swapped)
    return update(index, slab, both, both_other, keep, lead_other, right)


def solution(mesh):
    inner = Mesh(mesh.devices.reshape(X, Z, Y, CORE), ("x", "z", "y", "core"))
    spec = P(None, ("x", "z"), None, ("y", "core"))
    return jax.shard_map(per_device, mesh=inner, in_specs=(spec,), out_specs=spec, check_vma=False)
```

```python
import functools
import jax
import jax.numpy as jnp
from jax import lax
from jax.experimental import pallas as pl
from jax.experimental.pallas import tpu as pltpu
from jax.sharding import Mesh
from jax.sharding import PartitionSpec as P

NB = 256
STEP = 8
HALF = 128
X, Z, Y, CORE = 4, 8, 4, 2
RBL, CBL = 6, 4
PART = RBL // 2
PLANE = ("x", "y", "core")


def times_transposed(left, right):
    return lax.dot_general(
        left, right, (((1,), (1,)), ((), ())), preferred_element_type=jnp.float32
    )


def lane_of(tile, lane):
    return jnp.broadcast_to(tile[:, lane:lane + 1], (STEP, HALF))


def row_of(tile, row):
    return jnp.broadcast_to(tile[row:row + 1, :], tile.shape)


def symmetric(value):
    rows = lax.broadcasted_iota(jnp.int32, value.shape, 0)
    cols = lax.broadcasted_iota(jnp.int32, value.shape, 1)
    return jnp.where(rows >= cols, value, value.T)


def factor(work, inverse_ref, upper_ref):
    lanes = lax.broadcasted_iota(jnp.int32, (STEP, HALF), 1)
    rows = lax.broadcasted_iota(jnp.int32, (STEP, HALF), 0)
    for step in range(HALF // STEP):
        j = step * STEP
        tile = work[j:j + STEP, :]
        cols = [lane_of(tile, j + k) for k in range(STEP)]
        left = [[row_of(cols[k], s) if k <= s else None for k in range(STEP)] for s in range(STEP)]
        low = [[None] * STEP for _ in range(STEP)]
        root = [None] * STEP
        inside = (lanes >= j) & (lanes < j + STEP)
        right = [
            jnp.where(inside, jnp.where(lanes == j + i, 1.0, 0.0), row_of(tile, i)) for i in range(STEP)
        ]
        solved = [None] * STEP
        for k in range(STEP):
            root[k] = lax.rsqrt(left[k][k])
            for s in range(k + 1, STEP):
                low[s][k] = left[s][k] * root[k]
            for s in range(k + 1, STEP):
                for m in range(k + 1, s + 1):
                    left[s][m] = left[s][m] - low[s][k] * low[m][k]
            solved[k] = right[k] * root[k]
            for s in range(k + 1, STEP):
                right[s] = right[s] - low[s][k] * solved[k]
        if step + 1 < HALF // STEP:
            rest = work[j + STEP:j + 2 * STEP, :]
            ahead = [lane_of(rest, j + k) for k in range(STEP)]
            total = jnp.where(inside, 0.0, rest)
            for k in range(STEP):
                ahead[k] = ahead[k] * root[k]
                for s in range(k + 1, STEP):
                    ahead[s] = ahead[s] - ahead[k] * low[s][k]
                total = total - ahead[k] * solved[k]
            work[j + STEP:j + 2 * STEP, :] = total
        weights = [None] * STEP
        for i in range(STEP - 1, -1, -1):
            total = solved[i]
            for s in range(i + 1, STEP):
                total = total - low[s][i] * weights[s]
            weights[i] = total * root[i]
        for t in range(step + 2, HALF // STEP):
            other = work[t * STEP:(t + 1) * STEP, :]
            total = jnp.where(inside, 0.0, other)
            for i in range(STEP):
                total = total - lane_of(other, j + i) * weights[i]
            work[t * STEP:(t + 1) * STEP, :] = total
        final = solved[0]
        for i in range(1, STEP):
            final = jnp.where(rows == i, solved[i], final)
        block = jnp.zeros((STEP, HALF), jnp.float32)
        for i in range(STEP):
            for s in range(i, STEP):
                value = low[s][i] if s > i else left[i][i] * root[i]
                block = jnp.where((rows == i) & (lanes == j + s), value, block)
        inverse_ref[j:j + STEP, :] = jnp.where(lanes < j + STEP, final, 0.0)
        upper_ref[j:j + STEP, :] = jnp.where(lanes >= j + STEP, final, block)


def split(value):
    high = value.astype(jnp.bfloat16)
    rest = value - high.astype(jnp.float32)
    middle = rest.astype(jnp.bfloat16)
    return high, middle, (rest - middle.astype(jnp.float32)).astype(jnp.bfloat16)


def times_table(value, table):
    high, middle, low = split(value)
    wide = jnp.concatenate([high, high, high, middle, middle, low], axis=1)
    return jnp.dot(wide, table, preferred_element_type=jnp.float32)


def table_of(value):
    high, middle, low = split(value)
    return jnp.concatenate([high, middle, low, high, middle, high])


def leading_kernel(pieces, tables, lower, first_low, source, first_inverse, below, inverse, upper, work):
    for part in range(2):
        source[part] = pieces[:, 2 * part].reshape(NB, NB)
    work[...] = symmetric(source[0, :HALF, :HALF])
    zeros = jnp.zeros((HALF, HALF), jnp.float32)

    @pl.loop(0, 4)
    def _(part):
        panel = part // 2
        factor(work, inverse, upper)

        @pl.when(part % 2 == 0)
        def _():
            first_inverse[...] = inverse[...]
            side = times_table(source[panel, HALF:, :HALF], table_of(inverse[...].T))
            below[...] = side
            work[...] = symmetric(source[panel, HALF:, HALF:] - times_table(side, table_of(side.T)))
            lower[panel, :HALF, :HALF] = upper[...].T
            lower[panel, :HALF, HALF:] = zeros
            lower[panel, HALF:, :HALF] = side

        @pl.when(part % 2 == 1)
        def _():
            corner = times_table(below[...], table_of(first_inverse[...]))
            corner = -times_table(inverse[...], table_of(corner))
            top = jnp.concatenate([first_inverse[...].T, corner.T], axis=1)
            bottom = jnp.concatenate([zeros, inverse[...].T], axis=1)
            tables[panel] = table_of(jnp.concatenate([top, bottom]))
            lower[panel, HALF:, HALF:] = upper[...].T

        @pl.when(part == 1)
        def _():
            rows = times_table(pieces[:, 1].reshape(NB, NB), tables[0]).astype(jnp.bfloat16)
            first_low[...] = rows.T
            source[1] = source[1] - times_transposed(rows, rows)
            work[...] = symmetric(source[1, :HALF, :HALF])


def factor_leading(pieces):
    whole = pl.BlockSpec(memory_space=pltpu.VMEM)
    square = pltpu.VMEM((HALF, HALF), jnp.float32)
    return pl.pallas_call(
        leading_kernel,
        out_shape=[
            jax.ShapeDtypeStruct((2, 6 * NB, NB), jnp.bfloat16),
            pltpu.HBM((2, NB, NB), jnp.float32),
            jax.ShapeDtypeStruct((NB, NB), jnp.bfloat16),
        ],
        in_specs=[whole],
        out_specs=[whole] * 3,
        scratch_shapes=[pltpu.VMEM((2, NB, NB), jnp.float32)] + [square] * 5,
        compiler_params=pltpu.CompilerParams(vmem_limit_bytes=16 * 2**20),
        cost_estimate=pl.CostEstimate(flops=2**10, bytes_accessed=2**10, transcendentals=0),
        name="leading",
    )(pieces)


def panel_rows(raw_first, raw_second, tables, first_low):
    first = times_table(raw_first, tables[0])
    first_bf16 = first.astype(jnp.bfloat16)
    column = raw_second - jnp.dot(first_bf16, first_low[...], preferred_element_type=jnp.float32)
    second = times_table(column, tables[1])
    return first, first_bf16, second


def left_kernel(index, mine, other, tables, lower, first_low, both, keep, give):
    row_block = (index[2] * PART + pl.program_id(0)) * (X * Z) + index[0]
    swap = index[2] == 1
    raw_first = jnp.where(swap, other[0], mine[0])
    raw_second = jnp.where(swap, mine[0], other[0])
    first, first_bf16, second = panel_rows(raw_first, raw_second, tables, first_low)
    first = jnp.where(row_block == 0, lower[0], first)
    second = jnp.where(row_block == 1, lower[1], jnp.where(row_block == 0, 0.0, second))
    both[0, :, :NB] = first.astype(jnp.bfloat16)
    both[0, :, NB:] = second.astype(jnp.bfloat16)
    keep[0] = jnp.where(swap, second, first)
    give[0] = jnp.where(swap, first, second)


def fixed(*shape):
    return pl.BlockSpec(shape, lambda b, _: (0,) * len(shape))


def by_row(*shape):
    return pl.BlockSpec((1,) + shape, lambda b, _: (b,) + (0,) * len(shape))


def left_rows(index, mine, other, tables, lower, first_low):
    panel = pltpu.HBM((PART, NB, NB), jnp.float32)
    return pl.pallas_call(
        left_kernel,
        grid_spec=pltpu.PrefetchScalarGridSpec(
            num_scalar_prefetch=1,
            grid=(PART,),
            in_specs=[by_row(NB, NB)] * 2 + [fixed(2, 6 * NB, NB), fixed(2, NB, NB), fixed(NB, NB)],
            out_specs=[by_row(NB, 2 * NB), by_row(NB, NB), by_row(NB, NB)],
        ),
        out_shape=[pltpu.HBM((PART, NB, 2 * NB), jnp.bfloat16), panel, panel],
        compiler_params=pltpu.CompilerParams(vmem_limit_bytes=20 * 2**20),
        cost_estimate=pl.CostEstimate(flops=2**10, bytes_accessed=2**10, transcendentals=0),
        name="left_rows",
    )(index, mine, other, tables, in_hbm(lower), first_low)


def right_kernel(raw, tables, first_low, out):
    raw_first, raw_second = (raw[:, part].reshape(NB, NB) for part in range(2))
    _, first_bf16, second = panel_rows(raw_first, raw_second, tables, first_low)
    second_bf16 = second.astype(jnp.bfloat16)
    for device in range(X):
        out[device, :, :NB] = first_bf16
        out[device, :, NB:] = second_bf16


def right_rows(raw, tables, first_low):
    whole = pl.BlockSpec(memory_space=pltpu.VMEM)
    return pl.pallas_call(
        right_kernel,
        out_shape=pltpu.HBM((X, NB, 2 * NB), jnp.bfloat16),
        in_specs=[whole] * 3,
        out_specs=whole,
        compiler_params=pltpu.CompilerParams(vmem_limit_bytes=16 * 2**20),
        cost_estimate=pl.CostEstimate(flops=2**10, bytes_accessed=2**10, transcendentals=0),
        name="right_rows",
    )(raw, tables, first_low)


def update_kernel(index, slab, both_mine, both_other, lead_mine, lead_other, right, out):
    col_index = index[1]
    for part in range(2):
        own = index[2] == part
        row_block = (part * PART + pl.program_id(0)) * (X * Z) + index[0]
        both = jnp.where(own, both_mine[0], both_other[0])
        for m in range(CBL):
            change = times_transposed(both, right[m])
            live = (row_block >= 2) & (m * (Y * CORE) + col_index >= 2)
            value = slab[part, 0, :, m, :] - jnp.where(live, change, 0.0)
            if m == 0:
                lead = jnp.where(own, lead_mine[0], lead_other[0])
                value = jnp.where(col_index < 2, lead, value)
            out[part, 0, :, m, :] = value


def update(index, slab, both_mine, both_other, lead_mine, lead_other, right):
    halves = (2, PART) + slab.shape[1:]
    place = pl.BlockSpec((2, 1, NB, CBL, NB), lambda s, _: (0, s, 0, 0, 0))
    return pl.pallas_call(
        update_kernel,
        grid_spec=pltpu.PrefetchScalarGridSpec(
            num_scalar_prefetch=1,
            grid=(PART,),
            in_specs=[
                place, by_row(NB, 2 * NB), by_row(NB, 2 * NB), by_row(NB, NB), by_row(NB, NB),
                fixed(CBL, NB, 2 * NB),
            ],
            out_specs=place,
        ),
        out_shape=jax.ShapeDtypeStruct(halves, jnp.float32),
        compiler_params=pltpu.CompilerParams(vmem_limit_bytes=30 * 2**20),
        cost_estimate=pl.CostEstimate(flops=2**10, bytes_accessed=2**10, transcendentals=0),
        name="update",
    )(
        index, in_hbm(slab.reshape(halves)), in_hbm(both_mine), both_other, in_hbm(lead_mine),
        lead_other, right,
    ).reshape(slab.shape)


def in_hbm(value):
    return pltpu.with_memory_space_constraint(value, pltpu.HBM)


def tie(value, *others):
    return lax.optimization_barrier((value,) + others)[0]


def per_device(slab):
    x, z = lax.axis_index("x"), lax.axis_index("z")
    y, core = lax.axis_index("y"), lax.axis_index("core")
    column = y * CORE + core
    index = jnp.stack([x * Z + z, column, core]).astype(jnp.int32)
    top = slab[0, :, 0, :]
    chunk = NB // Z
    swapped = [(0, 1), (1, 0)]

    def half(which):
        rows = lax.dynamic_slice(slab, (which * PART, 0, 0, 0), (PART, NB, 1, NB))
        return rows.reshape(PART, NB, NB)

    mine_zero = half(core)

    def place(k):
        pairs = [(zz * Y * CORE + k, zz * Y * CORE + zz) for zz in range(Z)]
        return lax.ppermute(top, ("z", "y", "core"), pairs)

    scattered = lax.all_to_all(top.reshape(X * Y * CORE, STEP, NB), PLANE, 0, 0)[:2]
    scattered = tie(scattered, mine_zero)
    placed = jnp.stack([place(0), place(1)])
    to_z = jnp.concatenate(
        [
            jnp.broadcast_to(scattered.reshape(1, 2 * STEP, NB), (Z, 2 * STEP, NB)),
            placed.reshape(2, Z, chunk, NB).transpose(1, 0, 2, 3).reshape(Z, 2 * chunk, NB),
        ],
        axis=1,
    )
    other_zero = lax.ppermute(tie(half(1 - core), scattered), "core", swapped)
    zero = jnp.stack([mine_zero, other_zero])
    one = lax.ppermute(zero, "y", [(0, 1)])
    three = lax.ppermute(zero, "y", [(0, 3)])
    from_z = lax.all_to_all(to_z, "z", 0, 0)
    pieces = jnp.concatenate([from_z[0, :STEP], from_z[1, :2 * STEP]]).reshape(1, 3, STEP, NB)
    pieces = lax.all_to_all(
        jnp.broadcast_to(pieces, (X * Y * CORE, 3, STEP, NB)), PLANE, 0, 0
    )
    pieces = tie(pieces, one, three)
    two = lax.ppermute(one, "y", [(1, 2)])
    raw = lax.dynamic_index_in_dim(from_z[:, 2 * STEP:], column, 0).reshape(1, 2, chunk, NB)
    raw = jnp.broadcast_to(raw, (Z, 2, chunk, NB))
    raw = lax.all_to_all(tie(raw, pieces, one, three), "z", 0, 0)

    tables, lower, first_low = factor_leading(pieces)

    share = right_rows(raw, tables, first_low)
    right = lax.all_to_all(share, "x", 0, 0)

    zero, two = tie((zero, two), share)
    mine, other = (
        jnp.where(y == 0, zero[i], jnp.where(y == 1, one[i], jnp.where(y == 3, three[i], two[i])))
        for i in range(2)
    )
    both, keep, give = left_rows(index, mine, other, tables, lower, first_low)
    both_other = lax.ppermute(both, "core", swapped)
    lead_other = lax.ppermute(give, ("y", "core"), swapped)
    return update(index, slab, both, both_other, keep, lead_other, right)


def solution(mesh):
    inner = Mesh(mesh.devices.reshape(X, Z, Y, CORE), ("x", "z", "y", "core"))
    spec = P(None, ("x", "z"), None, ("y", "core"))
    return jax.shard_map(per_device, mesh=inner, in_specs=(spec,), out_specs=spec, check_vma=False)
```

```python
import functools
import jax
import jax.numpy as jnp
from jax import lax
from jax.experimental import pallas as pl
from jax.experimental.pallas import tpu as pltpu
from jax.sharding import Mesh
from jax.sharding import PartitionSpec as P

NB = 256
STEP = 8
HALF = 128
X, Z, Y, CORE = 4, 8, 4, 2
RBL, CBL = 6, 4
PART = RBL // 2
PLANE = ("x", "y", "core")


def times_transposed(left, right):
    return lax.dot_general(
        left, right, (((1,), (1,)), ((), ())), preferred_element_type=jnp.float32
    )


def lane_of(tile, lane):
    return jnp.broadcast_to(tile[:, lane:lane + 1], (STEP, HALF))


def row_of(tile, row):
    return jnp.broadcast_to(tile[row:row + 1, :], tile.shape)


def symmetric(value):
    rows = lax.broadcasted_iota(jnp.int32, value.shape, 0)
    cols = lax.broadcasted_iota(jnp.int32, value.shape, 1)
    return jnp.where(rows >= cols, value, value.T)


def factor(work, inverse_ref, upper_ref):
    lanes = lax.broadcasted_iota(jnp.int32, (STEP, HALF), 1)
    rows = lax.broadcasted_iota(jnp.int32, (STEP, HALF), 0)
    for step in range(HALF // STEP):
        j = step * STEP
        tile = work[j:j + STEP, :]
        cols = [lane_of(tile, j + k) for k in range(STEP)]
        left = [[row_of(cols[k], s) if k <= s else None for k in range(STEP)] for s in range(STEP)]
        low = [[None] * STEP for _ in range(STEP)]
        root = [None] * STEP
        inside = (lanes >= j) & (lanes < j + STEP)
        right = [
            jnp.where(inside, jnp.where(lanes == j + i, 1.0, 0.0), row_of(tile, i)) for i in range(STEP)
        ]
        solved = [None] * STEP
        for k in range(STEP):
            root[k] = lax.rsqrt(left[k][k])
            for s in range(k + 1, STEP):
                low[s][k] = left[s][k] * root[k]
            for s in range(k + 1, STEP):
                for m in range(k + 1, s + 1):
                    left[s][m] = left[s][m] - low[s][k] * low[m][k]
            solved[k] = right[k] * root[k]
            for s in range(k + 1, STEP):
                right[s] = right[s] - low[s][k] * solved[k]
        if step + 1 < HALF // STEP:
            rest = work[j + STEP:j + 2 * STEP, :]
            ahead = [lane_of(rest, j + k) for k in range(STEP)]
            total = jnp.where(inside, 0.0, rest)
            for k in range(STEP):
                ahead[k] = ahead[k] * root[k]
                for s in range(k + 1, STEP):
                    ahead[s] = ahead[s] - ahead[k] * low[s][k]
                total = total - ahead[k] * solved[k]
            work[j + STEP:j + 2 * STEP, :] = total
        weights = [None] * STEP
        for i in range(STEP - 1, -1, -1):
            total = solved[i]
            for s in range(i + 1, STEP):
                total = total - low[s][i] * weights[s]
            weights[i] = total * root[i]
        for t in range(step + 2, HALF // STEP):
            other = work[t * STEP:(t + 1) * STEP, :]
            total = jnp.where(inside, 0.0, other)
            for i in range(STEP):
                total = total - lane_of(other, j + i) * weights[i]
            work[t * STEP:(t + 1) * STEP, :] = total
        final = solved[0]
        for i in range(1, STEP):
            final = jnp.where(rows == i, solved[i], final)
        block = jnp.zeros((STEP, HALF), jnp.float32)
        for i in range(STEP):
            for s in range(i, STEP):
                value = low[s][i] if s > i else left[i][i] * root[i]
                block = jnp.where((rows == i) & (lanes == j + s), value, block)
        inverse_ref[j:j + STEP, :] = jnp.where(lanes < j + STEP, final, 0.0)
        upper_ref[j:j + STEP, :] = jnp.where(lanes >= j + STEP, final, block)


def split(value):
    high = value.astype(jnp.bfloat16)
    rest = value - high.astype(jnp.float32)
    middle = rest.astype(jnp.bfloat16)
    return high, middle, (rest - middle.astype(jnp.float32)).astype(jnp.bfloat16)


def times_table(value, table):
    high, middle, low = split(value)
    wide = jnp.concatenate([high, high, high, middle, middle, low], axis=1)
    return jnp.dot(wide, table, preferred_element_type=jnp.float32)


def table_of(value):
    high, middle, low = split(value)
    return jnp.concatenate([high, middle, low, high, middle, high])


def leading_kernel(pieces, tables, lower, first_low, source, first_inverse, below, inverse, upper, work):
    for part in range(2):
        source[part] = pieces[:, 2 * part].reshape(NB, NB)
    work[...] = symmetric(source[0, :HALF, :HALF])
    zeros = jnp.zeros((HALF, HALF), jnp.float32)

    @pl.loop(0, 4)
    def _(part):
        panel = part // 2
        factor(work, inverse, upper)

        @pl.when(part % 2 == 0)
        def _():
            first_inverse[...] = inverse[...]
            side = times_table(source[panel, HALF:, :HALF], table_of(inverse[...].T))
            below[...] = side
            work[...] = symmetric(source[panel, HALF:, HALF:] - times_table(side, table_of(side.T)))
            lower[panel, :HALF, :HALF] = upper[...].T
            lower[panel, :HALF, HALF:] = zeros
            lower[panel, HALF:, :HALF] = side

        @pl.when(part % 2 == 1)
        def _():
            corner = times_table(below[...], table_of(first_inverse[...]))
            corner = -times_table(inverse[...], table_of(corner))
            top = jnp.concatenate([first_inverse[...].T, corner.T], axis=1)
            bottom = jnp.concatenate([zeros, inverse[...].T], axis=1)
            tables[panel] = table_of(jnp.concatenate([top, bottom]))
            lower[panel, HALF:, HALF:] = upper[...].T

        @pl.when(part == 1)
        def _():
            rows = times_table(pieces[:, 1].reshape(NB, NB), tables[0]).astype(jnp.bfloat16)
            first_low[...] = rows.T
            source[1] = source[1] - times_transposed(rows, rows)
            work[...] = symmetric(source[1, :HALF, :HALF])


def factor_leading(pieces):
    whole = pl.BlockSpec(memory_space=pltpu.VMEM)
    square = pltpu.VMEM((HALF, HALF), jnp.float32)
    return pl.pallas_call(
        leading_kernel,
        out_shape=[
            jax.ShapeDtypeStruct((2, 6 * NB, NB), jnp.bfloat16),
            pltpu.HBM((2, NB, NB), jnp.float32),
            jax.ShapeDtypeStruct((NB, NB), jnp.bfloat16),
        ],
        in_specs=[whole],
        out_specs=[whole] * 3,
        scratch_shapes=[pltpu.VMEM((2, NB, NB), jnp.float32)] + [square] * 5,
        compiler_params=pltpu.CompilerParams(vmem_limit_bytes=16 * 2**20),
        cost_estimate=pl.CostEstimate(flops=2**10, bytes_accessed=2**10, transcendentals=0),
        name="leading",
    )(pieces)


def panel_rows(raw_first, raw_second, tables, first_low):
    first = times_table(raw_first, tables[0])
    first_bf16 = first.astype(jnp.bfloat16)
    column = raw_second - jnp.dot(first_bf16, first_low[...], preferred_element_type=jnp.float32)
    second = times_table(column, tables[1])
    return first, first_bf16, second


def left_kernel(index, mine, other, tables, lower, first_low, both, keep, give):
    row_block = (index[2] * PART + pl.program_id(0)) * (X * Z) + index[0]
    swap = index[2] == 1
    raw_first = jnp.where(swap, other[0], mine[0])
    raw_second = jnp.where(swap, mine[0], other[0])
    first, first_bf16, second = panel_rows(raw_first, raw_second, tables, first_low)
    first = jnp.where(row_block == 0, lower[0], first)
    second = jnp.where(row_block == 1, lower[1], jnp.where(row_block == 0, 0.0, second))
    both[0, :, :NB] = first.astype(jnp.bfloat16)
    both[0, :, NB:] = second.astype(jnp.bfloat16)
    keep[0] = jnp.where(swap, second, first)
    give[0] = jnp.where(swap, first, second)


def fixed(*shape):
    return pl.BlockSpec(shape, lambda b, _: (0,) * len(shape))


def by_row(*shape):
    return pl.BlockSpec((1,) + shape, lambda b, _: (b,) + (0,) * len(shape))


def left_rows(index, mine, other, tables, lower, first_low):
    panel = pltpu.HBM((PART, NB, NB), jnp.float32)
    return pl.pallas_call(
        left_kernel,
        grid_spec=pltpu.PrefetchScalarGridSpec(
            num_scalar_prefetch=1,
            grid=(PART,),
            in_specs=[by_row(NB, NB)] * 2 + [fixed(2, 6 * NB, NB), fixed(2, NB, NB), fixed(NB, NB)],
            out_specs=[by_row(NB, 2 * NB), by_row(NB, NB), by_row(NB, NB)],
        ),
        out_shape=[pltpu.HBM((PART, NB, 2 * NB), jnp.bfloat16), panel, panel],
        compiler_params=pltpu.CompilerParams(vmem_limit_bytes=20 * 2**20),
        cost_estimate=pl.CostEstimate(flops=2**10, bytes_accessed=2**10, transcendentals=0),
        name="left_rows",
    )(index, mine, other, tables, in_hbm(lower), first_low)


def right_kernel(raw, tables, first_low, out):
    raw_first, raw_second = (raw[:, part].reshape(NB, NB) for part in range(2))
    _, first_bf16, second = panel_rows(raw_first, raw_second, tables, first_low)
    second_bf16 = second.astype(jnp.bfloat16)
    for device in range(X):
        out[device, :, :NB] = first_bf16
        out[device, :, NB:] = second_bf16


def right_rows(raw, tables, first_low):
    whole = pl.BlockSpec(memory_space=pltpu.VMEM)
    return pl.pallas_call(
        right_kernel,
        out_shape=pltpu.HBM((X, NB, 2 * NB), jnp.bfloat16),
        in_specs=[whole] * 3,
        out_specs=whole,
        compiler_params=pltpu.CompilerParams(vmem_limit_bytes=16 * 2**20),
        cost_estimate=pl.CostEstimate(flops=2**10, bytes_accessed=2**10, transcendentals=0),
        name="right_rows",
    )(raw, tables, first_low)


def update_kernel(index, slab, both_mine, both_other, lead_mine, lead_other, right, out):
    col_index = index[1]
    swap = index[2] == 1
    both = jnp.concatenate(
        [jnp.where(swap, both_other[0], both_mine[0]), jnp.where(swap, both_mine[0], both_other[0])]
    )
    for m in range(CBL):
        change = times_transposed(both, right[m])
        for part in range(2):
            row_block = (part * PART + pl.program_id(0)) * (X * Z) + index[0]
            live = (row_block >= 2) & (m * (Y * CORE) + col_index >= 2)
            rows = change[part * NB:(part + 1) * NB]
            value = slab[part, 0, :, m, :] - jnp.where(live, rows, 0.0)
            if m == 0:
                lead = jnp.where(index[2] == part, lead_mine[0], lead_other[0])
                value = jnp.where(col_index < 2, lead, value)
            out[part, 0, :, m, :] = value


def update(index, slab, both_mine, both_other, lead_mine, lead_other, right):
    halves = (2, PART) + slab.shape[1:]
    place = pl.BlockSpec((2, 1, NB, CBL, NB), lambda s, _: (0, s, 0, 0, 0))
    return pl.pallas_call(
        update_kernel,
        grid_spec=pltpu.PrefetchScalarGridSpec(
            num_scalar_prefetch=1,
            grid=(PART,),
            in_specs=[
                place, by_row(NB, 2 * NB), by_row(NB, 2 * NB), by_row(NB, NB), by_row(NB, NB),
                fixed(CBL, NB, 2 * NB),
            ],
            out_specs=place,
        ),
        out_shape=jax.ShapeDtypeStruct(halves, jnp.float32),
        compiler_params=pltpu.CompilerParams(vmem_limit_bytes=30 * 2**20),
        cost_estimate=pl.CostEstimate(flops=2**10, bytes_accessed=2**10, transcendentals=0),
        name="update",
    )(
        index, in_hbm(slab.reshape(halves)), in_hbm(both_mine), both_other, in_hbm(lead_mine),
        lead_other, right,
    ).reshape(slab.shape)


def in_hbm(value):
    return pltpu.with_memory_space_constraint(value, pltpu.HBM)


def tie(value, *others):
    return lax.optimization_barrier((value,) + others)[0]


def per_device(slab):
    x, z = lax.axis_index("x"), lax.axis_index("z")
    y, core = lax.axis_index("y"), lax.axis_index("core")
    column = y * CORE + core
    index = jnp.stack([x * Z + z, column, core]).astype(jnp.int32)
    top = slab[0, :, 0, :]
    chunk = NB // Z
    swapped = [(0, 1), (1, 0)]

    def half(which):
        rows = lax.dynamic_slice(slab, (which * PART, 0, 0, 0), (PART, NB, 1, NB))
        return rows.reshape(PART, NB, NB)

    mine_zero = half(core)
    other_zero = lax.ppermute(half(1 - core), "core", swapped)

    def place(k):
        pairs = [(zz * Y * CORE + k, zz * Y * CORE + zz) for zz in range(Z)]
        return lax.ppermute(top, ("z", "y", "core"), pairs)

    scattered = lax.all_to_all(top.reshape(X * Y * CORE, STEP, NB), PLANE, 0, 0)[:2]
    scattered = tie(scattered, mine_zero)
    placed = jnp.stack([place(0), place(1)])
    to_z = jnp.concatenate(
        [
            jnp.broadcast_to(scattered.reshape(1, 2 * STEP, NB), (Z, 2 * STEP, NB)),
            placed.reshape(2, Z, chunk, NB).transpose(1, 0, 2, 3).reshape(Z, 2 * chunk, NB),
        ],
        axis=1,
    )
    mine_one = lax.ppermute(mine_zero, "y", [(0, 1)])
    mine_three = lax.ppermute(mine_zero, "y", [(0, 3)])
    from_z = lax.all_to_all(to_z, "z", 0, 0)
    from_z = tie(from_z, mine_one, mine_three, other_zero)
    pieces = jnp.concatenate([from_z[0, :STEP], from_z[1, :2 * STEP]]).reshape(1, 3, STEP, NB)
    other_one = lax.ppermute(other_zero, "y", [(0, 1)])
    other_three = lax.ppermute(other_zero, "y", [(0, 3)])
    mine_two = lax.ppermute(mine_one, "y", [(1, 2)])
    pieces = lax.all_to_all(
        jnp.broadcast_to(pieces, (X * Y * CORE, 3, STEP, NB)), PLANE, 0, 0
    )
    pieces = tie(pieces, other_one, other_three)
    other_two = lax.ppermute(other_three, "y", [(3, 2)])
    raw = lax.dynamic_index_in_dim(from_z[:, 2 * STEP:], column, 0).reshape(1, 2, chunk, NB)
    raw = jnp.broadcast_to(raw, (Z, 2, chunk, NB))
    raw = lax.all_to_all(tie(raw, pieces, other_one, other_three, mine_two), "z", 0, 0)

    tables, lower, first_low = factor_leading(pieces)

    share = right_rows(raw, tables, first_low)
    right = lax.all_to_all(share, "x", 0, 0)

    def select(zero, one, two, three):
        return jnp.where(y == 0, zero, jnp.where(y == 1, one, jnp.where(y == 3, three, two)))

    mine = select(mine_zero, mine_one, tie(mine_two, share), mine_three)
    other = select(other_zero, other_one, tie(other_two, share), other_three)
    both, keep, give = left_rows(index, mine, other, tables, lower, first_low)
    both_other = lax.ppermute(both, "core", swapped)
    lead_other = lax.ppermute(give, ("y", "core"), swapped)
    return update(index, slab, both, both_other, keep, lead_other, right)


def solution(mesh):
    inner = Mesh(mesh.devices.reshape(X, Z, Y, CORE), ("x", "z", "y", "core"))
    spec = P(None, ("x", "z"), None, ("y", "core"))
    return jax.shard_map(per_device, mesh=inner, in_specs=(spec,), out_specs=spec, check_vma=False)
```
